32 devices in a mesh: freq: 16 (over z, y, core), kpt: 2 (over x).
Axes of the slice: x: 2, y: 2, z: 4, core: 2. Of those that a mesh axis runs over, the one named last changes fastest.
Arguments:
- band_energy: float32 [2, 384], P('kpt'), may hold values from -4.5 to 4.5, as said below
- projector: bfloat16 [2, 640, 384], P('kpt', 'freq'), may hold values from -0.25 to 0.25
- sigma: float32 [2, 5, 5, 128, 16], P(None, None, None, 'freq'), may hold values from -8.5 to 8.5, as said below
- atom_of_slot: int32 [128], replicated, may hold values from 0 to 127, each once
- kweight: int32 [2], replicated, may hold values from 1 to 16
Outputs:
- local_green: float32 [2, 5, 5, 128, 16], P(None, None, None, ('freq', 'kpt'))
The draws below stay inside these ranges and needn't reach their ends.
Inputs may be any that keep to these rules, and one draw needn't show every extreme that they name: `band_energy`: every entry is a band energy; the energies of one k-point share a common offset drawn per k-point. Each block sigma[0, :, :, s, n] is symmetric; each block sigma[1, :, :, s, n] is symmetric and negative definite. `atom_of_slot`: A permutation of 0 to 127; slot s belongs to the owner s // (128 // 16) along freq.
All inputs are finite; a program needn't handle non-finite values.
Results may differ from the reference program's by a relative error of at most 0.0003.
Values may be sent and summed in bfloat16 or wider, within the bound.
A program may use at most 64 MiB of HBM per device.

```python
import math
import jax
import jax.numpy as jnp
from jax import lax

BANDS = 384
ATOMS = 128
ORBS = 5
ORBITALS = 640
KPOINTS = 2
FREQS = 16


def draw_band_energy(key, part):
    first, second = jax.random.split(jax.random.fold_in(key, 11))
    offset = jax.random.uniform(first, (KPOINTS, 1), jnp.float32, -2.0, 2.0)
    base = jax.random.uniform(second, (KPOINTS, BANDS), jnp.float32, -2.5, 2.5)
    return (offset + base).astype(jnp.float32)


def draw_sigma(key, part):
    first, second = jax.random.split(jax.random.fold_in(key, 23))
    shape = (ORBS, ORBS, ATOMS, FREQS)
    raw = jax.random.truncated_normal(first, -3.0, 3.0, shape, jnp.float32)
    factor = jax.random.truncated_normal(second, -3.0, 3.0, shape, jnp.float32)
    real_scale = 0.3
    imag_scale = 0.45
    real_part = real_scale * (raw + jnp.transpose(raw, (1, 0, 2, 3)))
    gram = jnp.einsum('mcaf,ocaf->moaf', factor, factor) / ORBS
    eye = jnp.eye(ORBS, dtype=jnp.float32)[:, :, None, None]
    imag_part = -(imag_scale * gram + 0.1 * eye)
    return jnp.stack([real_part, imag_part]).astype(jnp.float32)


def levels(key, dims, cuts, smallest, top_value):
    gain = 1.0
    for position, blocks in cuts:
        steps = jax.random.uniform(jax.random.fold_in(jax.random.fold_in(key, 6), position), (blocks,), jnp.float32, smallest / len(cuts), top_value / len(cuts))
        gain = gain * jnp.repeat(jnp.exp(steps), dims[position] // blocks).reshape((-1,) + (1,) * (len(dims) - 1 - position))
    return gain


def bell_draw(own_key, extent, width, reach, pieces=(), kind=jnp.bfloat16):
    entries = jax.random.normal(own_key, extent, jnp.float32) * width
    if len(pieces) > 0:
        entries = levels(own_key, extent, pieces, -0.22, 0.18) * entries
    return jnp.clip(entries, min=-reach, max=reach).astype(kind)


def setup_inputs(seed: int = 0) -> dict:
    key_of = jax.random.split(jax.random.key(seed), 6)
    band_energy = draw_band_energy(jax.random.fold_in(key_of[5], 71), 0)
    projector = bell_draw(key_of[1], (KPOINTS, ORBITALS, BANDS), ORBITALS ** -0.5, 0.25, ((0, 2), (1, 16)))
    sigma = draw_sigma(jax.random.fold_in(key_of[5], 71), 0)
    atom_of_slot = jax.random.permutation(key_of[3], ATOMS).astype(jnp.int32)
    kweight = jax.random.randint(key_of[4], (KPOINTS,), 1, 17).astype(jnp.int32)
    return dict(band_energy=band_energy, projector=projector, sigma=sigma, atom_of_slot=atom_of_slot, kweight=kweight)


HIGH = lax.Precision.HIGHEST
BETA_INV = 0.1

def local_block(energy, proj, real_sig, imag_sig, omega):
    proj3 = proj.reshape(ATOMS, ORBS, BANDS).astype(jnp.float32)
    real_rows = jnp.einsum('amo,aob->amb', real_sig, proj3, precision=HIGH).reshape(ATOMS * ORBS, BANDS).astype(jnp.bfloat16)
    imag_rows = jnp.einsum('amo,aob->amb', imag_sig, proj3, precision=HIGH).reshape(ATOMS * ORBS, BANDS).astype(jnp.bfloat16)
    up_real = jnp.dot(proj.T.astype(jnp.float32), real_rows.astype(jnp.float32), preferred_element_type=jnp.float32)
    up_imag = jnp.dot(proj.T.astype(jnp.float32), imag_rows.astype(jnp.float32), preferred_element_type=jnp.float32)
    eye = jnp.eye(BANDS, dtype=jnp.float32)
    x_mat = -jnp.diag(energy) - 0.5 * (up_real + up_real.T)
    y_mat = omega * eye - 0.5 * (up_imag + up_imag.T)
    lower = jnp.linalg.cholesky(y_mat)
    left = jax.scipy.linalg.solve_triangular(lower, x_mat, lower=True)
    core = jax.scipy.linalg.solve_triangular(lower, left.T, lower=True)
    core = 0.5 * (core + core.T)
    square = jnp.dot(core, core, precision=HIGH) + eye
    factor = jnp.linalg.cholesky(square)
    upper_rows = jax.scipy.linalg.solve_triangular(lower, proj.astype(jnp.float32).T, lower=True).T
    solved = jax.scipy.linalg.cho_solve((factor, True), upper_rows.T)
    wide = solved.T.reshape(ATOMS, ORBS, BANDS)
    turned = jnp.dot(upper_rows, core, precision=HIGH).reshape(ATOMS, ORBS, BANDS)
    real_part = jnp.einsum('amb,aob->amo', turned, wide, precision=HIGH)
    imag_part = -jnp.einsum('amb,aob->amo', upper_rows.reshape(ATOMS, ORBS, BANDS), wide, precision=HIGH)
    return jnp.stack([real_part, imag_part])

def reference(band_energy, projector, sigma, atom_of_slot, kweight):
    onehot = (atom_of_slot[:, None] == jnp.arange(ATOMS, dtype=jnp.int32)[None, :]).astype(jnp.float32)
    sig_atom = jnp.einsum('xmosf,sa->xmoaf', sigma, onehot, precision=HIGH)
    weights = kweight.astype(jnp.float32)
    total = jnp.sum(weights)

    def one_freq(index):
        omega = (2.0 * index.astype(jnp.float32) + 1.0) * math.pi * BETA_INV
        sig_now = lax.dynamic_index_in_dim(sig_atom, index, 4, keepdims=False)
        real_sig = jnp.transpose(sig_now[0], (2, 0, 1))
        imag_sig = jnp.transpose(sig_now[1], (2, 0, 1))

        def add_point(point, acc):
            block = local_block(band_energy[point], projector[point], real_sig, imag_sig, omega)
            return acc + weights[point] * block
        return lax.fori_loop(0, KPOINTS, add_point, jnp.zeros((2, ATOMS, ORBS, ORBS), jnp.float32))
    blocks = lax.map(one_freq, jnp.arange(FREQS, dtype=jnp.int32))
    slots = jnp.einsum('fxamo,sa->xmosf', blocks, onehot, precision=HIGH)
    return slots / total
```

```python
import functools
import math

import jax
import jax.numpy as jnp
from jax import lax
from jax.experimental import pallas as pl
from jax.experimental.pallas import tpu as pltpu
from jax.sharding import PartitionSpec as P

ORBS = 5
TILE = 128
STEP = 32

HIGH = lax.Precision.HIGHEST
BETA_INV = 0.1

OUTER = (((0,), (0,)), ((), ()))
ROWS = (((1,), (1,)), ((), ()))


def halves(value):
    top = value.astype(jnp.bfloat16)
    return top, (value - top.astype(jnp.float32)).astype(jnp.bfloat16)


def dot(a, b, dims=(((1,), (0,)), ((), ()))):
    return lax.dot_general(a, b, dims, preferred_element_type=jnp.float32)


def small_inverse(real, imag):
    size = real.shape[0]
    lanes = lax.broadcasted_iota(jnp.int32, (1, size), 1)
    rows = lax.broadcasted_iota(jnp.int32, (size, 1), 0)
    for k in range(size):
        here = lanes == k
        down = rows == k
        pr, pi = real[k : k + 1, k : k + 1], imag[k : k + 1, k : k + 1]
        scale = 1.0 / (pr * pr + pi * pi)
        qr, qi = pr * scale, -pi * scale
        cr = jnp.where(down, 1.0, real[:, k : k + 1])
        ci = jnp.where(down, 0.0, imag[:, k : k + 1])
        rr = jnp.where(here, 1.0, real[k : k + 1, :])
        ri = jnp.where(here, 0.0, imag[k : k + 1, :])
        sr = rr * qr - ri * qi
        si = rr * qi + ri * qr
        cross = here | down
        real = jnp.where(cross, 0.0, real) - (cr * sr - ci * si)
        imag = jnp.where(cross, 0.0, imag) - (cr * si + ci * sr)
    return real, imag


def sweep(mr, mi, bands):
    eye = (
        lax.broadcasted_iota(jnp.int32, (STEP, STEP), 0)
        == lax.broadcasted_iota(jnp.int32, (STEP, STEP), 1)
    ).astype(jnp.float32)
    lane = lax.broadcasted_iota(jnp.int32, (STEP, TILE), 1)
    row = lax.broadcasted_iota(jnp.int32, (STEP, TILE), 0)
    wide = lax.broadcasted_iota(jnp.int32, (1, bands), 1)

    def tile_step(tile, carry):
        base = pl.multiple_of(tile * TILE, TILE)
        for part in range(TILE // STEP):
            off = part * STEP
            start = pl.multiple_of(base + off, STEP)
            own = pl.ds(start, STEP)
            cols = pl.ds(base, TILE)
            dr = mr[own, cols][:, off : off + STEP]
            di = mi[own, cols][:, off : off + STEP]
            nr, ni = small_inverse(dr, di)
            vr, vi = -nr, -ni
            place = wide - start
            inside = (place >= 0) & (place < STEP)
            unit = (
                lax.broadcasted_iota(jnp.int32, (STEP, bands), 1)
                == lax.broadcasted_iota(jnp.int32, (STEP, bands), 0) + start
            ).astype(jnp.float32)
            rr = jnp.where(inside, unit, mr[own, :])
            ri = jnp.where(inside, 0.0, mi[own, :])
            rrh, rrl = halves(rr)
            rih, ril = halves(ri)
            stack = jnp.concatenate([rrh, rrh, rrl, rih, rih, ril], axis=0)
            vrh, vrl = halves(vr)
            vih, vil = halves(vi)
            left = jnp.concatenate(
                [
                    jnp.concatenate([vrh, vrl, vrh, -vih, -vil, -vih], axis=0),
                    jnp.concatenate([vih, vil, vih, vrh, vrl, vrh], axis=0),
                ],
                axis=1,
            )
            both = dot(left, stack, OUTER)
            qr, qi = both[:STEP], both[STEP:]
            qrh, qrl = halves(qr)
            qih, qil = halves(qi)
            to_real = jnp.concatenate([qrh, qrl, qrh, -qih, -qil, -qih], axis=0)
            to_imag = jnp.concatenate([qih, qil, qih, qrh, qrl, qrh], axis=0)
            mr[...] = jnp.where(inside, 0.0, mr[...]) - dot(stack, to_real, OUTER)
            mi[...] = jnp.where(inside, 0.0, mi[...]) - dot(stack, to_imag, OUTER)
            mr[own, :] = -qr
            mi[own, :] = -qi
        return carry

    lax.fori_loop(0, bands // TILE, tile_step, 0)


def point_kernel(scalars, proj_ref, sig_ref, slot_ref, energy_ref, out_ref, mr, mi, pm):
    atoms = slot_ref.shape[1]
    orbitals, bands = proj_ref.shape
    omega, weight = scalars[0], scalars[1]
    rows = lax.broadcasted_iota(jnp.int32, (atoms, atoms), 0)
    cols = lax.broadcasted_iota(jnp.int32, (atoms, atoms), 1)
    eye = rows == cols
    turn = (rows == slot_ref[...]).astype(jnp.float32)
    sig = lax.dot_general(sig_ref[...], turn, ROWS, precision=HIGH, preferred_element_type=jnp.float32)

    proj = proj_ref[...]
    orow = lax.broadcasted_iota(jnp.int32, (atoms, orbitals), 0)
    ocol = lax.broadcasted_iota(jnp.int32, (atoms, orbitals), 1)
    for m in range(ORBS):
        pick = (ocol == orow * ORBS + m).astype(jnp.float32).astype(jnp.bfloat16)
        pm[m * atoms : (m + 1) * atoms, :] = dot(pick, proj).astype(jnp.bfloat16)
    planes = pm[...]

    def lifted(first):
        made = []
        for m in range(ORBS):
            line = [
                jnp.where(eye, sig[first + m * ORBS + o : first + m * ORBS + o + 1, :], 0.0)
                for o in range(ORBS)
            ]
            high, low = halves(jnp.concatenate(line, axis=1))
            made.append((dot(high, planes) + dot(low, planes)).astype(jnp.bfloat16))
        made = jnp.concatenate(made, axis=0)
        return dot(
            jnp.concatenate([planes, made], axis=0), jnp.concatenate([made, planes], axis=0), OUTER
        )

    diag = lax.broadcasted_iota(jnp.int32, (bands, bands), 0) == lax.broadcasted_iota(
        jnp.int32, (bands, bands), 1
    )
    mr[...] = -jnp.where(diag, energy_ref[...], 0.0) - 0.5 * lifted(0)
    mi[...] = jnp.where(diag, omega, 0.0) - 0.5 * lifted(ORBS * ORBS)

    sweep(mr, mi, bands)

    lines = []
    for ref in (mr, mi):
        high, low = halves(ref[...])
        spread = dot(planes, high) + dot(planes, low)
        for m in range(ORBS):
            vh, vl = halves(spread[m * atoms : (m + 1) * atoms, :])
            block = dot(vh, planes, ROWS) + dot(vl, planes, ROWS)
            for o in range(ORBS):
                lines.append(
                    jnp.sum(
                        jnp.where(eye, block[:, o * atoms : (o + 1) * atoms], 0.0),
                        axis=0,
                        keepdims=True,
                    )
                )
    found = jnp.concatenate(lines, axis=0) * (-weight)
    out_ref[...] = jnp.dot(found, turn, precision=HIGH, preferred_element_type=jnp.float32)


def point_blocks(scalars, proj, sig, slots, energy, **options):
    orbitals, bands = proj.shape
    vmem = pl.BlockSpec(memory_space=pltpu.VMEM)
    return pl.pallas_call(
        point_kernel,
        out_shape=jax.ShapeDtypeStruct(sig.shape, jnp.float32),
        in_specs=[pl.BlockSpec(memory_space=pltpu.SMEM)] + [vmem] * 4,
        out_specs=vmem,
        scratch_shapes=[
            pltpu.VMEM((bands, bands), jnp.float32),
            pltpu.VMEM((bands, bands), jnp.float32),
            pltpu.VMEM((orbitals, bands), jnp.bfloat16),
        ],
        compiler_params=pltpu.CompilerParams(vmem_limit_bytes=56 * 1024 * 1024),
        name="point",
        **options,
    )(scalars, proj, sig, slots, energy)


def local(band_energy, projector, sigma, atom_of_slot, kweight):
    freq_count = lax.axis_size("freq")
    freq_index = lax.axis_index("freq")
    kpt_index = lax.axis_index("kpt")
    points = band_energy.shape[0]
    atoms = atom_of_slot.shape[0]
    per_freq = sigma.shape[4] // freq_count
    projections = lax.all_gather(projector, "freq", axis=1, tiled=True)
    sig_here = lax.all_to_all(sigma, "freq", split_axis=4, concat_axis=3, tiled=True)
    weights = kweight.astype(jnp.float32)
    total = jnp.sum(weights)
    own_weights = lax.dynamic_slice_in_dim(weights, kpt_index * points, points, 0)
    slots = atom_of_slot.reshape(1, atoms)

    columns = []
    for here in range(per_freq):
        number = freq_index * per_freq + here
        omega = (2.0 * number.astype(jnp.float32) + 1.0) * math.pi * BETA_INV
        sig = sig_here[..., here].reshape(2 * ORBS * ORBS, atoms)
        summed = 0.0
        for point in range(points):
            scalars = jnp.stack([omega, own_weights[point] / total])
            summed = summed + point_blocks(
                scalars, projections[point], sig, slots, band_energy[point : point + 1]
            )
        columns.append(summed.reshape(2, ORBS, ORBS, atoms))
    partial_blocks = jnp.stack(columns, axis=4)
    owned = lax.all_to_all(partial_blocks, "freq", split_axis=3, concat_axis=4, tiled=True)
    return lax.psum_scatter(owned, "kpt", scatter_dimension=3, tiled=True)


def solution(mesh):
    placed = (P("kpt", None), P("kpt", "freq", None), P(None, None, None, "freq", None), P(), P())
    return jax.shard_map(
        local,
        mesh=mesh,
        in_specs=placed,
        out_specs=P(None, None, None, ("freq", "kpt"), None),
        check_vma=False,
    )
```

```python
import functools
import math

import jax
import jax.numpy as jnp
from jax import lax
from jax.experimental import pallas as pl
from jax.experimental.pallas import tpu as pltpu
from jax.sharding import PartitionSpec as P

ORBS = 5
TILE = 128
MESH = pl.DeviceIdType.MESH
STEP = 32

HIGH = lax.Precision.HIGHEST
BETA_INV = 0.1

OUTER = (((0,), (0,)), ((), ()))
ROWS = (((1,), (1,)), ((), ()))


def halves(value):
    top = value.astype(jnp.bfloat16)
    return top, (value - top.astype(jnp.float32)).astype(jnp.bfloat16)


def dot(a, b, dims=(((1,), (0,)), ((), ()))):
    return lax.dot_general(a, b, dims, preferred_element_type=jnp.float32)


def small_inverse(real, imag):
    size = real.shape[0]
    lanes = lax.broadcasted_iota(jnp.int32, (1, size), 1)
    rows = lax.broadcasted_iota(jnp.int32, (size, 1), 0)
    for k in range(size):
        here = lanes == k
        down = rows == k
        pr, pi = real[k : k + 1, k : k + 1], imag[k : k + 1, k : k + 1]
        scale = 1.0 / (pr * pr + pi * pi)
        qr, qi = pr * scale, -pi * scale
        cr = jnp.where(down, 1.0, real[:, k : k + 1])
        ci = jnp.where(down, 0.0, imag[:, k : k + 1])
        rr = jnp.where(here, 1.0, real[k : k + 1, :])
        ri = jnp.where(here, 0.0, imag[k : k + 1, :])
        sr = rr * qr - ri * qi
        si = rr * qi + ri * qr
        cross = here | down
        real = jnp.where(cross, 0.0, real) - (cr * sr - ci * si)
        imag = jnp.where(cross, 0.0, imag) - (cr * si + ci * sr)
    return real, imag


def sweep(mr, mi, bands):
    eye = (
        lax.broadcasted_iota(jnp.int32, (STEP, STEP), 0)
        == lax.broadcasted_iota(jnp.int32, (STEP, STEP), 1)
    ).astype(jnp.float32)
    lane = lax.broadcasted_iota(jnp.int32, (STEP, TILE), 1)
    row = lax.broadcasted_iota(jnp.int32, (STEP, TILE), 0)
    wide = lax.broadcasted_iota(jnp.int32, (1, bands), 1)

    def tile_step(tile, carry):
        base = pl.multiple_of(tile * TILE, TILE)
        for part in range(TILE // STEP):
            off = part * STEP
            start = pl.multiple_of(base + off, STEP)
            own = pl.ds(start, STEP)
            cols = pl.ds(base, TILE)
            dr = mr[own, cols][:, off : off + STEP]
            di = mi[own, cols][:, off : off + STEP]
            nr, ni = small_inverse(dr, di)
            vr, vi = -nr, -ni
            place = wide - start
            inside = (place >= 0) & (place < STEP)
            unit = (
                lax.broadcasted_iota(jnp.int32, (STEP, bands), 1)
                == lax.broadcasted_iota(jnp.int32, (STEP, bands), 0) + start
            ).astype(jnp.float32)
            rr = jnp.where(inside, unit, mr[own, :])
            ri = jnp.where(inside, 0.0, mi[own, :])
            rrh, rrl = halves(rr)
            rih, ril = halves(ri)
            stack = jnp.concatenate([rrh, rrh, rrl, rih, rih, ril], axis=0)
            vrh, vrl = halves(vr)
            vih, vil = halves(vi)
            left = jnp.concatenate(
                [
                    jnp.concatenate([vrh, vrl, vrh, -vih, -vil, -vih], axis=0),
                    jnp.concatenate([vih, vil, vih, vrh, vrl, vrh], axis=0),
                ],
                axis=1,
            )
            both = dot(left, stack, OUTER)
            qr, qi = both[:STEP], both[STEP:]
            qrh, qrl = halves(qr)
            qih, qil = halves(qi)
            to_real = jnp.concatenate([qrh, qrl, qrh, -qih, -qil, -qih], axis=0)
            to_imag = jnp.concatenate([qih, qil, qih, qrh, qrl, qrh], axis=0)
            mr[...] = jnp.where(inside, 0.0, mr[...]) - dot(stack, to_real, OUTER)
            mi[...] = jnp.where(inside, 0.0, mi[...]) - dot(stack, to_imag, OUTER)
            mr[own, :] = -qr
            mi[own, :] = -qi
        return carry

    lax.fori_loop(0, bands // TILE, tile_step, 0)


def point_kernel(point, points, kweight, proj_ref, sig_ref, slot_ref, back_ref, energy_ref, out_ref, mr, mi, pm):
    atoms = slot_ref.shape[1]
    owners, padded, bands = proj_ref.shape
    each = atoms // owners
    omega = (2 * lax.axis_index("freq") + 1).astype(jnp.float32) * (math.pi * BETA_INV)
    count = kweight.shape[0]
    total = sum(kweight[i] for i in range(count)).astype(jnp.float32)
    weight = kweight[lax.axis_index("kpt") * points + point].astype(jnp.float32)
    rows = lax.broadcasted_iota(jnp.int32, (atoms, atoms), 0)
    cols = lax.broadcasted_iota(jnp.int32, (atoms, atoms), 1)
    eye = rows == cols
    turn = (rows == slot_ref[...]).astype(jnp.float32)
    sig = jnp.dot(turn, sig_ref[...], precision=HIGH, preferred_element_type=jnp.float32).T

    proj = proj_ref[...].reshape(owners * padded, bands)
    orow = lax.broadcasted_iota(jnp.int32, (atoms, owners * padded), 0)
    ocol = lax.broadcasted_iota(jnp.int32, (atoms, owners * padded), 1)
    target = ocol - (lax.div(orow, each) * padded + lax.rem(orow, each) * ORBS)
    for m in range(ORBS):
        pick = (target == m).astype(jnp.float32).astype(jnp.bfloat16)
        pm[m * atoms : (m + 1) * atoms, :] = dot(pick, proj).astype(jnp.bfloat16)
    planes = pm[...]

    def lifted(first):
        made = []
        for m in range(ORBS):
            line = [
                jnp.where(eye, sig[first + m * ORBS + o : first + m * ORBS + o + 1, :], 0.0)
                for o in range(ORBS)
            ]
            high, low = halves(jnp.concatenate(line, axis=1))
            made.append((dot(high, planes) + dot(low, planes)).astype(jnp.bfloat16))
        made = jnp.concatenate(made, axis=0)
        return dot(
            jnp.concatenate([planes, made], axis=0), jnp.concatenate([made, planes], axis=0), OUTER
        )

    diag = lax.broadcasted_iota(jnp.int32, (bands, bands), 0) == lax.broadcasted_iota(
        jnp.int32, (bands, bands), 1
    )
    mr[...] = -jnp.where(diag, energy_ref[...], 0.0) - 0.5 * lifted(0)
    mi[...] = jnp.where(diag, omega, 0.0) - 0.5 * lifted(ORBS * ORBS)

    sweep(mr, mi, bands)

    lines = []
    for ref in (mr, mi):
        high, low = halves(ref[...])
        spread = dot(planes, high) + dot(planes, low)
        for m in range(ORBS):
            vh, vl = halves(spread[m * atoms : (m + 1) * atoms, :])
            block = dot(vh, planes, ROWS) + dot(vl, planes, ROWS)
            for o in range(ORBS):
                lines.append(
                    jnp.sum(
                        jnp.where(eye, block[:, o * atoms : (o + 1) * atoms], 0.0),
                        axis=0,
                        keepdims=True,
                    )
                )
    scale = jnp.full((1, 1), weight) / jnp.full((1, 1), total)
    found = jnp.concatenate(lines, axis=0) * -scale
    back = (rows == back_ref[...]).astype(jnp.float32)
    out_ref[...] = jnp.dot(found, back, precision=HIGH, preferred_element_type=jnp.float32).T


def point_blocks(point, points, kweight, proj, sig, slots, back, energy):
    owners, padded, bands = proj.shape
    atoms = slots.shape[1]
    vmem = pl.BlockSpec(memory_space=pltpu.VMEM)
    return pl.pallas_call(
        functools.partial(point_kernel, point, points),
        out_shape=jax.ShapeDtypeStruct(sig.shape, jnp.float32),
        in_specs=[pl.BlockSpec(memory_space=pltpu.SMEM)] + [vmem] * 5,
        out_specs=vmem,
        scratch_shapes=[
            pltpu.VMEM((bands, bands), jnp.float32),
            pltpu.VMEM((bands, bands), jnp.float32),
            pltpu.VMEM((ORBS * atoms, bands), jnp.bfloat16),
        ],
        compiler_params=pltpu.CompilerParams(vmem_limit_bytes=56 * 1024 * 1024),
        name="point",
    )(kweight, proj, sig, slots, back, energy)


def radices(count):
    made = []
    for radix in (2, 2):
        if count % radix == 0:
            made.insert(0, radix)
            count //= radix
    while count > 1:
        radix = 4 if count % 4 == 0 else count
        made.insert(0, radix)
        count //= radix
    return made


def greet(axis):
    count, me = lax.axis_size(axis), lax.axis_index(axis)
    barrier = pltpu.get_barrier_semaphore()
    for j in range(1, count):
        pl.semaphore_signal(
            barrier, inc=1, device_id={axis: lax.rem(me + j, count)}, device_id_type=MESH
        )
    return barrier, count - 1


def gather_kernel(proj_ref, sig_ref, proj_out, sig_out, proj_send, proj_recv, sig_send, sig_recv):
    count, me = lax.axis_size("freq"), lax.axis_index("freq")
    barrier, peers = greet("freq")
    points, rows, bands = proj_ref.shape
    padded = proj_out.shape[2]
    own = proj_ref[...]
    if padded > rows:
        own = jnp.concatenate([own, jnp.zeros((points, padded - rows, bands), own.dtype)], axis=1)
    proj_out[me] = own
    sig_out[me] = sig_ref[me]
    pl.semaphore_wait(barrier, peers)

    dims = radices(count)
    strides = [math.prod(dims[s + 1 :]) for s in range(len(dims))]

    def shifted(index, s, j):
        digit = lax.rem(lax.div(index, strides[s]), dims[s])
        return index + (lax.rem(digit + j, dims[s]) - digit) * strides[s]

    def block(owner, target, slot):
        return pltpu.make_async_remote_copy(
            src_ref=proj_out.at[owner],
            dst_ref=proj_out.at[owner],
            send_sem=proj_send.at[slot],
            recv_sem=proj_recv.at[owner],
            device_id={"freq": target},
            device_id_type=MESH,
        )

    sent = []

    def forward(owner, first):
        for s in range(first, len(dims)):
            for j in range(1, dims[s]):
                copy = block(owner, shifted(me, s, j), len(sent))
                copy.start()
                sent.append(copy)

    forward(me, 0)
    parts = []
    for j in range(1, count):
        target = lax.rem(me + j, count)
        copy = pltpu.make_async_remote_copy(
            src_ref=sig_ref.at[target],
            dst_ref=sig_out.at[me],
            send_sem=sig_send.at[j],
            recv_sem=sig_recv.at[me],
            device_id={"freq": target},
            device_id_type=MESH,
        )
        copy.start()
        parts.append(copy)
    got = [me]
    for s in range(len(dims)):
        fresh = []
        for j in range(1, dims[s]):
            for base in got:
                owner = shifted(base, s, j)
                block(owner, owner, 0).wait_recv()
                forward(owner, s + 1)
                fresh.append(owner)
        got += fresh
    for j in range(1, count):
        source = lax.rem(me + j, count)
        pltpu.make_async_remote_copy(
            src_ref=sig_ref.at[source],
            dst_ref=sig_out.at[source],
            send_sem=sig_send.at[j],
            recv_sem=sig_recv.at[source],
            device_id={"freq": source},
            device_id_type=MESH,
        ).wait_recv()
    for copy in sent + parts:
        copy.wait_send()


def gather(proj, sig, count):
    points, rows, bands = proj.shape
    padded = -(-rows // 16) * 16
    vmem = pl.BlockSpec(memory_space=pltpu.VMEM)
    return pl.pallas_call(
        gather_kernel,
        out_shape=(
            jax.ShapeDtypeStruct((count, points, padded, bands), proj.dtype),
            jax.ShapeDtypeStruct(sig.shape, sig.dtype),
        ),
        in_specs=[vmem, vmem],
        out_specs=(vmem, vmem),
        scratch_shapes=[pltpu.SemaphoreType.DMA((count,))] * 4,
        compiler_params=pltpu.CompilerParams(
            collective_id=0, has_side_effects=True, vmem_limit_bytes=32 * 1024 * 1024
        ),
        name="gather",
    )(proj, sig)


def exchange_kernel(mine_ref, out_ref, theirs, summed, kpt_sems, freq_send, freq_recv):
    count, me = lax.axis_size("freq"), lax.axis_index("freq")
    others, point = lax.axis_size("kpt"), lax.axis_index("kpt")
    _, peers = greet("freq")
    barrier, more = greet("kpt")
    pl.semaphore_wait(barrier, peers + more)
    kpt_send, kpt_recv = kpt_sems.at[0], kpt_sems.at[1]
    copies = []
    for j in range(1, others):
        target = lax.rem(point + j, others)
        copy = pltpu.make_async_remote_copy(
            src_ref=mine_ref.at[target],
            dst_ref=theirs.at[j],
            send_sem=kpt_send.at[j],
            recv_sem=kpt_recv.at[j],
            device_id={"kpt": target},
            device_id_type=MESH,
        )
        copy.start()
        copies.append(copy)
    total = mine_ref[point]
    for j in range(1, others):
        copies[j - 1].wait()
        total = total + theirs[j]
    each = summed.shape[1]
    for owner in range(count):
        summed[owner] = total[owner * each : (owner + 1) * each]
    copies = []
    for j in range(1, count):
        target = lax.rem(me + j, count)
        copy = pltpu.make_async_remote_copy(
            src_ref=summed.at[target],
            dst_ref=out_ref.at[me],
            send_sem=freq_send.at[j],
            recv_sem=freq_recv.at[me],
            device_id={"freq": target},
            device_id_type=MESH,
        )
        copy.start()
        copies.append(copy)
    out_ref[me] = summed[me]
    for j in range(1, count):
        source = lax.rem(me + j, count)
        pltpu.make_async_remote_copy(
            src_ref=summed.at[source],
            dst_ref=out_ref.at[source],
            send_sem=freq_send.at[j],
            recv_sem=freq_recv.at[source],
            device_id={"freq": source},
            device_id_type=MESH,
        ).wait_recv()
    for copy in copies:
        copy.wait_send()


def exchange(blocks, count, others):
    atoms, kinds = blocks.shape
    each = atoms // (count * others)
    vmem = pl.BlockSpec(memory_space=pltpu.VMEM)
    return pl.pallas_call(
        exchange_kernel,
        out_shape=jax.ShapeDtypeStruct((count, each, kinds), blocks.dtype),
        in_specs=[vmem],
        out_specs=vmem,
        scratch_shapes=[
            pltpu.VMEM((others, atoms // others, kinds), blocks.dtype),
            pltpu.VMEM((count, each, kinds), blocks.dtype),
            pltpu.SemaphoreType.DMA((2, others)),
            pltpu.SemaphoreType.DMA((count,)),
            pltpu.SemaphoreType.DMA((count,)),
        ],
        compiler_params=pltpu.CompilerParams(collective_id=1, has_side_effects=True),
        name="exchange",
    )(blocks.reshape(others, atoms // others, kinds))


def local(band_energy, projector, sigma, atom_of_slot, kweight):
    count, others = lax.axis_size("freq"), lax.axis_size("kpt")
    points = band_energy.shape[0]
    atoms = atom_of_slot.shape[0]
    kinds = 2 * ORBS * ORBS
    slots = sigma.shape[3]
    sig = jnp.transpose(sigma.reshape(kinds, slots, count), (2, 1, 0))
    projections, sig = gather(projector, sig, count)
    sig = sig.reshape(atoms, kinds)
    order = atom_of_slot.reshape(count, others, -1).transpose(1, 0, 2).reshape(1, atoms)
    summed = None
    for point in range(points):
        block = point_blocks(
            point,
            points,
            kweight,
            projections[:, point],
            sig,
            atom_of_slot.reshape(1, atoms),
            order,
            band_energy[point : point + 1],
        )
        summed = block if summed is None else summed + block
    owned = exchange(summed, count, others)
    return jnp.transpose(owned, (2, 1, 0)).reshape(2, ORBS, ORBS, -1, count)


def solution(mesh):
    placed = (P("kpt", None), P("kpt", "freq", None), P(None, None, None, "freq", None), P(), P())
    return jax.shard_map(
        local,
        mesh=mesh,
        in_specs=placed,
        out_specs=P(None, None, None, ("freq", "kpt"), None),
        check_vma=False,
    )
```

```python
import functools
import math

import jax
import jax.numpy as jnp
from jax import lax
from jax.experimental import pallas as pl
from jax.experimental.pallas import tpu as pltpu
from jax.sharding import PartitionSpec as P

ORBS = 5
TILE = 128
MESH = pl.DeviceIdType.MESH
STEP = 32

HIGH = lax.Precision.HIGHEST
BETA_INV = 0.1

OUTER = (((0,), (0,)), ((), ()))
ROWS = (((1,), (1,)), ((), ()))


def halves(value):
    top = value.astype(jnp.bfloat16)
    return top, (value - top.astype(jnp.float32)).astype(jnp.bfloat16)


def dot(a, b, dims=(((1,), (0,)), ((), ()))):
    return lax.dot_general(a, b, dims, preferred_element_type=jnp.float32)


def times(a, b):
    return a[0] * b[0] - a[1] * b[1], a[0] * b[1] + a[1] * b[0]


def plus(a, b):
    return a[0] + b[0], a[1] + b[1]


def minus(a, b):
    return a[0] - b[0], a[1] - b[1]


def pair_inverse(a, b, d):
    det = minus(times(a, d), times(b, b))
    scale = 1.0 / (det[0] * det[0] + det[1] * det[1])
    turned = (det[0] * scale, -det[1] * scale)
    low = times(b, turned)
    return times(d, turned), (-low[0], -low[1]), times(a, turned)


def quad_inverse(e):
    a, b, d = pair_inverse(e[0][0], e[1][0], e[1][1])
    t = [[plus(times(x, e[j][0]), times(y, e[j][1])) for j in (2, 3)] for x, y in ((a, b), (b, d))]
    rest = {}
    for i in (2, 3):
        for j in (2, 3):
            if j <= i:
                taken = plus(times(e[i][0], t[0][j - 2]), times(e[i][1], t[1][j - 2]))
                rest[i, j] = minus(e[i][j], taken)
    f, g, h = pair_inverse(rest[2, 2], rest[3, 2], rest[3, 3])
    n = [[plus(times(p[0], x), times(p[1], y)) for x, y in ((f, g), (g, h))] for p in t]
    top = [
        plus(a, plus(times(n[0][0], t[0][0]), times(n[0][1], t[0][1]))),
        plus(b, plus(times(n[0][0], t[1][0]), times(n[0][1], t[1][1]))),
        plus(d, plus(times(n[1][0], t[1][0]), times(n[1][1], t[1][1]))),
    ]
    neg = [[(-x[0], -x[1]) for x in line] for line in n]
    return [
        [top[0], top[1], neg[0][0], neg[0][1]],
        [top[1], top[2], neg[1][0], neg[1][1]],
        [neg[0][0], neg[1][0], f, g],
        [neg[0][1], neg[1][1], g, h],
    ]


def small_inverse(real, imag):
    size = real.shape[0]
    shape = (8, size)
    lanes = lax.broadcasted_iota(jnp.int32, shape, 1)
    rows = lax.broadcasted_iota(jnp.int32, shape, 0)
    parts = [
        [(m[h : h + 8, :]) for m in (real, imag)] for h in range(0, size, 8)
    ]
    for k in range(0, size, 4):
        own, off = k // 8, k % 8
        here = (lanes >= k) & (lanes < k + 4)
        down = (rows >= off) & (rows < off + 4)
        cols = [
            [
                tuple(jnp.broadcast_to(m[:, k + j : k + j + 1], shape) for m in part)
                for part in parts
            ]
            for j in range(4)
        ]
        e = [
            [
                tuple(jnp.broadcast_to(m[off + i : off + i + 1, :], shape) for m in cols[j][own])
                for j in range(i + 1)
            ]
            for i in range(4)
        ]
        line = []
        for i in range(4):
            r, v = (jnp.broadcast_to(m[off + i : off + i + 1, :], shape) for m in parts[own])
            line.append(
                (
                    jnp.where(here, (lanes == k + i).astype(jnp.float32), r),
                    jnp.where(here, 0.0, v),
                )
            )
        inverse = quad_inverse(e)
        solved = []
        for i in range(4):
            value = times(inverse[i][0], line[0])
            for j in range(1, 4):
                value = plus(value, times(inverse[i][j], line[j]))
            solved.append(value)
        fresh = []
        for h, part in enumerate(parts):
            gone = here | down if h == own else here
            value = tuple(jnp.where(gone, 0.0, m) for m in part)
            for j in range(4):
                col = cols[j][h]
                if h == own:
                    col = (
                        jnp.where(down, (rows == off + j).astype(jnp.float32), col[0]),
                        jnp.where(down, 0.0, col[1]),
                    )
                value = minus(value, times(col, solved[j]))
            fresh.append(value)
        parts = fresh
    return tuple(jnp.concatenate([p[x] for p in parts], axis=0) for x in range(2))


def sweep(mr, mi, bands):
    eye = (
        lax.broadcasted_iota(jnp.int32, (STEP, STEP), 0)
        == lax.broadcasted_iota(jnp.int32, (STEP, STEP), 1)
    ).astype(jnp.float32)
    lane = lax.broadcasted_iota(jnp.int32, (STEP, TILE), 1)
    row = lax.broadcasted_iota(jnp.int32, (STEP, TILE), 0)
    wide = lax.broadcasted_iota(jnp.int32, (1, bands), 1)

    def tile_step(tile, carry):
        base = pl.multiple_of(tile * TILE, TILE)
        for part in range(TILE // STEP):
            off = part * STEP
            start = pl.multiple_of(base + off, STEP)
            own = pl.ds(start, STEP)
            cols = pl.ds(base, TILE)
            dr = mr[own, cols][:, off : off + STEP]
            di = mi[own, cols][:, off : off + STEP]
            nr, ni = small_inverse(dr, di)
            vr, vi = -nr, -ni
            place = wide - start
            inside = (place >= 0) & (place < STEP)
            unit = (
                lax.broadcasted_iota(jnp.int32, (STEP, bands), 1)
                == lax.broadcasted_iota(jnp.int32, (STEP, bands), 0) + start
            ).astype(jnp.float32)
            rr = jnp.where(inside, unit, mr[own, :])
            ri = jnp.where(inside, 0.0, mi[own, :])
            rrh, rrl = halves(rr)
            rih, ril = halves(ri)
            stack = jnp.concatenate([rrh, rrh, rrl, rih, rih, ril], axis=0)
            vrh, vrl = halves(vr)
            vih, vil = halves(vi)
            left = jnp.concatenate(
                [
                    jnp.concatenate([vrh, vrl, vrh, -vih, -vil, -vih], axis=0),
                    jnp.concatenate([vih, vil, vih, vrh, vrl, vrh], axis=0),
                ],
                axis=1,
            )
            both = dot(left, stack, OUTER)
            qr, qi = both[:STEP], both[STEP:]
            qrh, qrl = halves(qr)
            qih, qil = halves(qi)
            to_real = jnp.concatenate([qrh, qrl, qrh, -qih, -qil, -qih], axis=0)
            to_imag = jnp.concatenate([qih, qil, qih, qrh, qrl, qrh], axis=0)
            mr[...] = jnp.where(inside, 0.0, mr[...]) - dot(stack, to_real, OUTER)
            mi[...] = jnp.where(inside, 0.0, mi[...]) - dot(stack, to_imag, OUTER)
            mr[own, :] = -qr
            mi[own, :] = -qi
        return carry

    lax.fori_loop(0, bands // TILE, tile_step, 0)


def point_kernel(point, points, kweight, proj_ref, sig_ref, slot_ref, back_ref, energy_ref, out_ref, mr, mi, pm):
    atoms = slot_ref.shape[1]
    owners, padded, bands = proj_ref.shape
    each = atoms // owners
    omega = (2 * lax.axis_index("freq") + 1).astype(jnp.float32) * (math.pi * BETA_INV)
    count = kweight.shape[0]
    total = sum(kweight[i] for i in range(count)).astype(jnp.float32)
    weight = kweight[lax.axis_index("kpt") * points + point].astype(jnp.float32)
    rows = lax.broadcasted_iota(jnp.int32, (atoms, atoms), 0)
    cols = lax.broadcasted_iota(jnp.int32, (atoms, atoms), 1)
    eye = rows == cols
    turn = (rows == slot_ref[...]).astype(jnp.float32)
    sig = jnp.dot(turn, sig_ref[...], precision=HIGH, preferred_element_type=jnp.float32).T

    proj = proj_ref[...].reshape(owners * padded, bands)
    orow = lax.broadcasted_iota(jnp.int32, (atoms, owners * padded), 0)
    ocol = lax.broadcasted_iota(jnp.int32, (atoms, owners * padded), 1)
    target = ocol - (lax.div(orow, each) * padded + lax.rem(orow, each) * ORBS)
    for m in range(ORBS):
        pick = (target == m).astype(jnp.float32).astype(jnp.bfloat16)
        pm[m * atoms : (m + 1) * atoms, :] = dot(pick, proj).astype(jnp.bfloat16)
    planes = pm[...]

    def lifted(first):
        made = []
        for m in range(ORBS):
            line = [
                jnp.where(eye, sig[first + m * ORBS + o : first + m * ORBS + o + 1, :], 0.0)
                for o in range(ORBS)
            ]
            high, low = halves(jnp.concatenate(line, axis=1))
            made.append((dot(high, planes) + dot(low, planes)).astype(jnp.bfloat16))
        made = jnp.concatenate(made, axis=0)
        return dot(
            jnp.concatenate([planes, made], axis=0), jnp.concatenate([made, planes], axis=0), OUTER
        )

    diag = lax.broadcasted_iota(jnp.int32, (bands, bands), 0) == lax.broadcasted_iota(
        jnp.int32, (bands, bands), 1
    )
    mr[...] = -jnp.where(diag, energy_ref[...], 0.0) - 0.5 * lifted(0)
    mi[...] = jnp.where(diag, omega, 0.0) - 0.5 * lifted(ORBS * ORBS)

    sweep(mr, mi, bands)

    lines = {}
    for which, ref in enumerate((mr, mi)):
        high, low = halves(ref[...])
        spread = dot(planes, high) + dot(planes, low)
        for m in range(ORBS):
            vh, vl = halves(spread[m * atoms : (m + 1) * atoms, :])
            rest = planes[m * atoms :, :]
            block = dot(vh, rest, ROWS) + dot(vl, rest, ROWS)
            for o in range(m, ORBS):
                part = block[:, (o - m) * atoms : (o - m + 1) * atoms]
                lines[which, m, o] = lines[which, o, m] = jnp.sum(
                    jnp.where(eye, part, 0.0), axis=0, keepdims=True
                )
    lines = [lines[w, m, o] for w in range(2) for m in range(ORBS) for o in range(ORBS)]
    scale = jnp.full((1, 1), weight) / jnp.full((1, 1), total)
    found = jnp.concatenate(lines, axis=0) * -scale
    back = (rows == back_ref[...]).astype(jnp.float32)
    out_ref[...] = jnp.dot(found, back, precision=HIGH, preferred_element_type=jnp.float32).T


def point_blocks(point, points, kweight, proj, sig, slots, back, energy):
    owners, padded, bands = proj.shape
    atoms = slots.shape[1]
    vmem = pl.BlockSpec(memory_space=pltpu.VMEM)
    return pl.pallas_call(
        functools.partial(point_kernel, point, points),
        out_shape=jax.ShapeDtypeStruct(sig.shape, jnp.float32),
        in_specs=[pl.BlockSpec(memory_space=pltpu.SMEM)] + [vmem] * 5,
        out_specs=vmem,
        scratch_shapes=[
            pltpu.VMEM((bands, bands), jnp.float32),
            pltpu.VMEM((bands, bands), jnp.float32),
            pltpu.VMEM((ORBS * atoms, bands), jnp.bfloat16),
        ],
        compiler_params=pltpu.CompilerParams(vmem_limit_bytes=56 * 1024 * 1024),
        name="point",
    )(kweight, proj, sig, slots, back, energy)


def radices(count):
    made = []
    for radix in (2, 2):
        if count % radix == 0:
            made.insert(0, radix)
            count //= radix
    while count > 1:
        radix = 4 if count % 4 == 0 else count
        made.insert(0, radix)
        count //= radix
    return made


def greet(axis):
    count, me = lax.axis_size(axis), lax.axis_index(axis)
    barrier = pltpu.get_barrier_semaphore()
    for j in range(1, count):
        pl.semaphore_signal(
            barrier, inc=1, device_id={axis: lax.rem(me + j, count)}, device_id_type=MESH
        )
    return barrier, count - 1


def gather_kernel(proj_ref, sig_ref, proj_out, sig_out, proj_send, proj_recv, sig_send, sig_recv):
    count, me = lax.axis_size("freq"), lax.axis_index("freq")
    barrier, peers = greet("freq")
    points, rows, bands = proj_ref.shape
    padded = proj_out.shape[2]
    own = proj_ref[...]
    if padded > rows:
        own = jnp.concatenate([own, jnp.zeros((points, padded - rows, bands), own.dtype)], axis=1)
    proj_out[me] = own
    sig_out[me] = sig_ref[me]
    pl.semaphore_wait(barrier, peers)

    dims = radices(count)
    strides = [math.prod(dims[s + 1 :]) for s in range(len(dims))]

    def shifted(index, s, j):
        digit = lax.rem(lax.div(index, strides[s]), dims[s])
        return index + (lax.rem(digit + j, dims[s]) - digit) * strides[s]

    def block(owner, target, slot):
        return pltpu.make_async_remote_copy(
            src_ref=proj_out.at[owner],
            dst_ref=proj_out.at[owner],
            send_sem=proj_send.at[slot],
            recv_sem=proj_recv.at[owner],
            device_id={"freq": target},
            device_id_type=MESH,
        )

    sent = []

    def forward(owner, first):
        for s in range(first, len(dims)):
            for j in range(1, dims[s]):
                copy = block(owner, shifted(me, s, j), len(sent))
                copy.start()
                sent.append(copy)

    forward(me, 0)
    parts = []
    for j in range(1, count):
        target = lax.rem(me + j, count)
        copy = pltpu.make_async_remote_copy(
            src_ref=sig_ref.at[target],
            dst_ref=sig_out.at[me],
            send_sem=sig_send.at[j],
            recv_sem=sig_recv.at[me],
            device_id={"freq": target},
            device_id_type=MESH,
        )
        copy.start()
        parts.append(copy)
    got = [me]
    for s in range(len(dims)):
        fresh = []
        for j in range(1, dims[s]):
            for base in got:
                owner = shifted(base, s, j)
                block(owner, owner, 0).wait_recv()
                forward(owner, s + 1)
                fresh.append(owner)
        got += fresh
    for j in range(1, count):
        source = lax.rem(me + j, count)
        pltpu.make_async_remote_copy(
            src_ref=sig_ref.at[source],
            dst_ref=sig_out.at[source],
            send_sem=sig_send.at[j],
            recv_sem=sig_recv.at[source],
            device_id={"freq": source},
            device_id_type=MESH,
        ).wait_recv()
    for copy in sent + parts:
        copy.wait_send()


def gather(proj, sig, count):
    points, rows, bands = proj.shape
    padded = -(-rows // 16) * 16
    vmem = pl.BlockSpec(memory_space=pltpu.VMEM)
    return pl.pallas_call(
        gather_kernel,
        out_shape=(
            jax.ShapeDtypeStruct((count, points, padded, bands), proj.dtype),
            jax.ShapeDtypeStruct(sig.shape, sig.dtype),
        ),
        in_specs=[vmem, vmem],
        out_specs=(vmem, vmem),
        scratch_shapes=[pltpu.SemaphoreType.DMA((count,))] * 4,
        compiler_params=pltpu.CompilerParams(
            collective_id=0, has_side_effects=True, vmem_limit_bytes=32 * 1024 * 1024
        ),
        name="gather",
    )(proj, sig)


def exchange_kernel(mine_ref, out_ref, theirs, summed, kpt_sems, freq_send, freq_recv):
    count, me = lax.axis_size("freq"), lax.axis_index("freq")
    others, point = lax.axis_size("kpt"), lax.axis_index("kpt")
    _, peers = greet("freq")
    barrier, more = greet("kpt")
    pl.semaphore_wait(barrier, peers + more)
    kpt_send, kpt_recv = kpt_sems.at[0], kpt_sems.at[1]
    copies = []
    for j in range(1, others):
        target = lax.rem(point + j, others)
        copy = pltpu.make_async_remote_copy(
            src_ref=mine_ref.at[target],
            dst_ref=theirs.at[j],
            send_sem=kpt_send.at[j],
            recv_sem=kpt_recv.at[j],
            device_id={"kpt": target},
            device_id_type=MESH,
        )
        copy.start()
        copies.append(copy)
    total = mine_ref[point]
    for j in range(1, others):
        copies[j - 1].wait()
        total = total + theirs[j]
    each = summed.shape[1]
    for owner in range(count):
        summed[owner] = total[owner * each : (owner + 1) * each]
    copies = []
    for j in range(1, count):
        target = lax.rem(me + j, count)
        copy = pltpu.make_async_remote_copy(
            src_ref=summed.at[target],
            dst_ref=out_ref.at[me],
            send_sem=freq_send.at[j],
            recv_sem=freq_recv.at[me],
            device_id={"freq": target},
            device_id_type=MESH,
        )
        copy.start()
        copies.append(copy)
    out_ref[me] = summed[me]
    for j in range(1, count):
        source = lax.rem(me + j, count)
        pltpu.make_async_remote_copy(
            src_ref=summed.at[source],
            dst_ref=out_ref.at[source],
            send_sem=freq_send.at[j],
            recv_sem=freq_recv.at[source],
            device_id={"freq": source},
            device_id_type=MESH,
        ).wait_recv()
    for copy in copies:
        copy.wait_send()


def exchange(blocks, count, others):
    atoms, kinds = blocks.shape
    each = atoms // (count * others)
    vmem = pl.BlockSpec(memory_space=pltpu.VMEM)
    return pl.pallas_call(
        exchange_kernel,
        out_shape=jax.ShapeDtypeStruct((count, each, kinds), blocks.dtype),
        in_specs=[vmem],
        out_specs=vmem,
        scratch_shapes=[
            pltpu.VMEM((others, atoms // others, kinds), blocks.dtype),
            pltpu.VMEM((count, each, kinds), blocks.dtype),
            pltpu.SemaphoreType.DMA((2, others)),
            pltpu.SemaphoreType.DMA((count,)),
            pltpu.SemaphoreType.DMA((count,)),
        ],
        compiler_params=pltpu.CompilerParams(collective_id=1, has_side_effects=True),
        name="exchange",
    )(blocks.reshape(others, atoms // others, kinds))


def local(band_energy, projector, sigma, atom_of_slot, kweight):
    count, others = lax.axis_size("freq"), lax.axis_size("kpt")
    points = band_energy.shape[0]
    atoms = atom_of_slot.shape[0]
    kinds = 2 * ORBS * ORBS
    slots = sigma.shape[3]
    sig = jnp.transpose(sigma.reshape(kinds, slots, count), (2, 1, 0))
    projections, sig = gather(projector, sig, count)
    sig = sig.reshape(atoms, kinds)
    order = atom_of_slot.reshape(count, others, -1).transpose(1, 0, 2).reshape(1, atoms)
    summed = None
    for point in range(points):
        block = point_blocks(
            point,
            points,
            kweight,
            projections[:, point],
            sig,
            atom_of_slot.reshape(1, atoms),
            order,
            band_energy[point : point + 1],
        )
        summed = block if summed is None else summed + block
    owned = exchange(summed, count, others)
    return jnp.transpose(owned, (2, 1, 0)).reshape(2, ORBS, ORBS, -1, count)


def solution(mesh):
    placed = (P("kpt", None), P("kpt", "freq", None), P(None, None, None, "freq", None), P(), P())
    return jax.shard_map(
        local,
        mesh=mesh,
        in_specs=placed,
        out_specs=P(None, None, None, ("freq", "kpt"), None),
        check_vma=False,
    )
```

```python
import functools
import math

import jax
import jax.numpy as jnp
from jax import lax
from jax.experimental import pallas as pl
from jax.experimental.pallas import tpu as pltpu
from jax.sharding import PartitionSpec as P

ORBS = 5
TILE = 128
MESH = pl.DeviceIdType.MESH
STEP = 32

HIGH = lax.Precision.HIGHEST
BETA_INV = 0.1

OUTER = (((0,), (0,)), ((), ()))
ROWS = (((1,), (1,)), ((), ()))


def halves(value):
    top = value.astype(jnp.bfloat16)
    return top, (value - top.astype(jnp.float32)).astype(jnp.bfloat16)


def dot(a, b, dims=(((1,), (0,)), ((), ()))):
    return lax.dot_general(a, b, dims, preferred_element_type=jnp.float32)


def times(a, b):
    return a[0] * b[0] - a[1] * b[1], a[0] * b[1] + a[1] * b[0]


def plus(a, b):
    return a[0] + b[0], a[1] + b[1]


def minus(a, b):
    return a[0] - b[0], a[1] - b[1]


def pair_inverse(a, b, d):
    det = minus(times(a, d), times(b, b))
    scale = 1.0 / (det[0] * det[0] + det[1] * det[1])
    turned = (det[0] * scale, -det[1] * scale)
    low = times(b, turned)
    return times(d, turned), (-low[0], -low[1]), times(a, turned)


def quad_inverse(e):
    a, b, d = pair_inverse(e[0][0], e[1][0], e[1][1])
    t = [[plus(times(x, e[j][0]), times(y, e[j][1])) for j in (2, 3)] for x, y in ((a, b), (b, d))]
    rest = {}
    for i in (2, 3):
        for j in (2, 3):
            if j <= i:
                taken = plus(times(e[i][0], t[0][j - 2]), times(e[i][1], t[1][j - 2]))
                rest[i, j] = minus(e[i][j], taken)
    f, g, h = pair_inverse(rest[2, 2], rest[3, 2], rest[3, 3])
    n = [[plus(times(p[0], x), times(p[1], y)) for x, y in ((f, g), (g, h))] for p in t]
    top = [
        plus(a, plus(times(n[0][0], t[0][0]), times(n[0][1], t[0][1]))),
        plus(b, plus(times(n[0][0], t[1][0]), times(n[0][1], t[1][1]))),
        plus(d, plus(times(n[1][0], t[1][0]), times(n[1][1], t[1][1]))),
    ]
    neg = [[(-x[0], -x[1]) for x in line] for line in n]
    return [
        [top[0], top[1], neg[0][0], neg[0][1]],
        [top[1], top[2], neg[1][0], neg[1][1]],
        [neg[0][0], neg[1][0], f, g],
        [neg[0][1], neg[1][1], g, h],
    ]


def small_inverse(real, imag):
    size = real.shape[0]
    shape = (8, size)
    lanes = lax.broadcasted_iota(jnp.int32, shape, 1)
    rows = lax.broadcasted_iota(jnp.int32, shape, 0)
    parts = [
        [(m[h : h + 8, :]) for m in (real, imag)] for h in range(0, size, 8)
    ]
    for k in range(0, size, 4):
        own, off = k // 8, k % 8
        here = (lanes >= k) & (lanes < k + 4)
        down = (rows >= off) & (rows < off + 4)
        cols = [
            [
                tuple(jnp.broadcast_to(m[:, k + j : k + j + 1], shape) for m in part)
                for part in parts
            ]
            for j in range(4)
        ]
        e = [
            [
                tuple(jnp.broadcast_to(m[off + i : off + i + 1, :], shape) for m in cols[j][own])
                for j in range(i + 1)
            ]
            for i in range(4)
        ]
        line = []
        for i in range(4):
            r, v = (jnp.broadcast_to(m[off + i : off + i + 1, :], shape) for m in parts[own])
            line.append(
                (
                    jnp.where(here, (lanes == k + i).astype(jnp.float32), r),
                    jnp.where(here, 0.0, v),
                )
            )
        inverse = quad_inverse(e)
        solved = []
        for i in range(4):
            value = times(inverse[i][0], line[0])
            for j in range(1, 4):
                value = plus(value, times(inverse[i][j], line[j]))
            solved.append(value)
        fresh = []
        for h, part in enumerate(parts):
            gone = here | down if h == own else here
            value = tuple(jnp.where(gone, 0.0, m) for m in part)
            for j in range(4):
                col = cols[j][h]
                if h == own:
                    col = (
                        jnp.where(down, (rows == off + j).astype(jnp.float32), col[0]),
                        jnp.where(down, 0.0, col[1]),
                    )
                value = minus(value, times(col, solved[j]))
            fresh.append(value)
        parts = fresh
    return tuple(jnp.concatenate([p[x] for p in parts], axis=0) for x in range(2))


def sweep(mr, mi, bands):
    eye = (
        lax.broadcasted_iota(jnp.int32, (STEP, STEP), 0)
        == lax.broadcasted_iota(jnp.int32, (STEP, STEP), 1)
    ).astype(jnp.float32)
    lane = lax.broadcasted_iota(jnp.int32, (STEP, TILE), 1)
    row = lax.broadcasted_iota(jnp.int32, (STEP, TILE), 0)
    wide = lax.broadcasted_iota(jnp.int32, (1, bands), 1)

    def tile_step(tile, carry):
        base = pl.multiple_of(tile * TILE, TILE)
        for part in range(TILE // STEP):
            off = part * STEP
            start = pl.multiple_of(base + off, STEP)
            own = pl.ds(start, STEP)
            cols = pl.ds(base, TILE)
            dr = mr[own, cols][:, off : off + STEP]
            di = mi[own, cols][:, off : off + STEP]
            nr, ni = small_inverse(dr, di)
            vr, vi = -nr, -ni
            place = wide - start
            inside = (place >= 0) & (place < STEP)
            unit = (
                lax.broadcasted_iota(jnp.int32, (STEP, bands), 1)
                == lax.broadcasted_iota(jnp.int32, (STEP, bands), 0) + start
            ).astype(jnp.float32)
            rr = jnp.where(inside, unit, mr[own, :])
            ri = jnp.where(inside, 0.0, mi[own, :])
            rrh, rrl = halves(rr)
            rih, ril = halves(ri)
            stack = jnp.concatenate([rrh, rrh, rrl, rih, rih, ril], axis=0)
            vrh, vrl = halves(vr)
            vih, vil = halves(vi)
            left = jnp.concatenate(
                [
                    jnp.concatenate([vrh, vrl, vrh, -vih, -vil, -vih], axis=0),
                    jnp.concatenate([vih, vil, vih, vrh, vrl, vrh], axis=0),
                ],
                axis=1,
            )
            both = dot(left, stack, OUTER)
            qr, qi = both[:STEP], both[STEP:]
            qrh, qrl = halves(qr)
            qih, qil = halves(qi)
            to_real = jnp.concatenate([qrh, qrl, qrh, -qih, -qil, -qih], axis=0)
            to_imag = jnp.concatenate([qih, qil, qih, qrh, qrl, qrh], axis=0)
            mr[...] = jnp.where(inside, 0.0, mr[...]) - dot(stack, to_real, OUTER)
            mi[...] = jnp.where(inside, 0.0, mi[...]) - dot(stack, to_imag, OUTER)
            mr[own, :] = -qr
            mi[own, :] = -qi
        return carry

    lax.fori_loop(0, bands // TILE, tile_step, 0)


def point_blocks(point, points, kweight, proj, sig_all, slot_ref, back_ref, energy_ref, mr, mi, pm):
    atoms = back_ref.shape[1]
    owners, padded, bands = proj.shape
    each = atoms // owners
    omega = (2 * lax.axis_index("freq") + 1).astype(jnp.float32) * (math.pi * BETA_INV)
    count = kweight.shape[0]
    total = sum(kweight[i] for i in range(count)).astype(jnp.float32)
    weight = kweight[lax.axis_index("kpt") * points + point].astype(jnp.float32)
    rows = lax.broadcasted_iota(jnp.int32, (atoms, atoms), 0)
    cols = lax.broadcasted_iota(jnp.int32, (atoms, atoms), 1)
    eye = rows == cols
    held = slot_ref.shape[1]
    turn = (lax.broadcasted_iota(jnp.int32, (atoms, held), 0) == slot_ref[...]).astype(jnp.float32)
    sig = sig_all[...].reshape(held, sig_all.shape[2])
    sig = jnp.dot(turn, sig, precision=HIGH, preferred_element_type=jnp.float32).T

    proj = proj.reshape(owners * padded, bands)
    orow = lax.broadcasted_iota(jnp.int32, (atoms, owners * padded), 0)
    ocol = lax.broadcasted_iota(jnp.int32, (atoms, owners * padded), 1)
    target = ocol - (lax.div(orow, each) * padded + lax.rem(orow, each) * ORBS)
    for m in range(ORBS):
        pick = (target == m).astype(jnp.float32).astype(jnp.bfloat16)
        pm[m * atoms : (m + 1) * atoms, :] = dot(pick, proj).astype(jnp.bfloat16)
    planes = pm[...]

    def lifted(first):
        made = []
        for m in range(ORBS):
            line = [
                jnp.where(eye, sig[first + m * ORBS + o : first + m * ORBS + o + 1, :], 0.0)
                for o in range(ORBS)
            ]
            high, low = halves(jnp.concatenate(line, axis=1))
            made.append((dot(high, planes) + dot(low, planes)).astype(jnp.bfloat16))
        made = jnp.concatenate(made, axis=0)
        return dot(
            jnp.concatenate([planes, made], axis=0), jnp.concatenate([made, planes], axis=0), OUTER
        )

    diag = lax.broadcasted_iota(jnp.int32, (bands, bands), 0) == lax.broadcasted_iota(
        jnp.int32, (bands, bands), 1
    )
    mr[...] = -jnp.where(diag, energy_ref[point : point + 1, :], 0.0) - 0.5 * lifted(0)
    mi[...] = jnp.where(diag, omega, 0.0) - 0.5 * lifted(ORBS * ORBS)

    sweep(mr, mi, bands)

    lines = {}
    for which, ref in enumerate((mr, mi)):
        high, low = halves(ref[...])
        spread = dot(planes, high) + dot(planes, low)
        for m in range(ORBS):
            vh, vl = halves(spread[m * atoms : (m + 1) * atoms, :])
            rest = planes[m * atoms :, :]
            block = dot(vh, rest, ROWS) + dot(vl, rest, ROWS)
            for o in range(m, ORBS):
                part = block[:, (o - m) * atoms : (o - m + 1) * atoms]
                lines[which, m, o] = lines[which, o, m] = jnp.sum(
                    jnp.where(eye, part, 0.0), axis=0, keepdims=True
                )
    lines = [lines[w, m, o] for w in range(2) for m in range(ORBS) for o in range(ORBS)]
    scale = jnp.full((1, 1), weight) / jnp.full((1, 1), total)
    found = jnp.concatenate(lines, axis=0) * -scale
    back = (rows == back_ref[...]).astype(jnp.float32)
    return jnp.dot(found, back, precision=HIGH, preferred_element_type=jnp.float32).T


def radices(count):
    made = []
    for radix in (2, 2):
        if count % radix == 0:
            made.insert(0, radix)
            count //= radix
    while count > 1:
        radix = 4 if count % 4 == 0 else count
        made.insert(0, radix)
        count //= radix
    return made


def greet(barrier, axis):
    count, me = lax.axis_size(axis), lax.axis_index(axis)
    for j in range(1, count):
        pl.semaphore_signal(
            barrier, inc=1, device_id={axis: lax.rem(me + j, count)}, device_id_type=MESH
        )
    return count - 1


def gather(proj_ref, sig_ref, proj_out, sig_out, proj_send, proj_recv, sig_send, sig_recv):
    count, me = lax.axis_size("freq"), lax.axis_index("freq")
    barrier = pltpu.get_barrier_semaphore()
    peers = greet(barrier, "freq") + greet(barrier, "kpt")
    points, rows, bands = proj_ref.shape
    padded = proj_out.shape[2]
    own = proj_ref[...]
    if padded > rows:
        own = jnp.concatenate([own, jnp.zeros((points, padded - rows, bands), own.dtype)], axis=1)
    proj_out[me] = own
    sig_out[me] = sig_ref[me]
    pl.semaphore_wait(barrier, peers)

    dims = radices(count)
    strides = [math.prod(dims[s + 1 :]) for s in range(len(dims))]

    def shifted(index, s, j):
        digit = lax.rem(lax.div(index, strides[s]), dims[s])
        return index + (lax.rem(digit + j, dims[s]) - digit) * strides[s]

    def block(owner, target, slot):
        return pltpu.make_async_remote_copy(
            src_ref=proj_out.at[owner],
            dst_ref=proj_out.at[owner],
            send_sem=proj_send.at[slot],
            recv_sem=proj_recv.at[owner],
            device_id={"freq": target},
            device_id_type=MESH,
        )

    sent = []

    def forward(owner, first):
        for s in range(first, len(dims)):
            for j in range(1, dims[s]):
                copy = block(owner, shifted(me, s, j), len(sent))
                copy.start()
                sent.append(copy)

    forward(me, 0)
    parts = []
    for j in range(1, count):
        target = lax.rem(me + j, count)
        copy = pltpu.make_async_remote_copy(
            src_ref=sig_ref.at[target],
            dst_ref=sig_out.at[me],
            send_sem=sig_send.at[j],
            recv_sem=sig_recv.at[me],
            device_id={"freq": target},
            device_id_type=MESH,
        )
        copy.start()
        parts.append(copy)
    got = [me]
    for s in range(len(dims)):
        fresh = []
        for j in range(1, dims[s]):
            for base in got:
                owner = shifted(base, s, j)
                block(owner, owner, 0).wait_recv()
                forward(owner, s + 1)
                fresh.append(owner)
        got += fresh
    for j in range(1, count):
        source = lax.rem(me + j, count)
        pltpu.make_async_remote_copy(
            src_ref=sig_ref.at[source],
            dst_ref=sig_out.at[source],
            send_sem=sig_send.at[j],
            recv_sem=sig_recv.at[source],
            device_id={"freq": source},
            device_id_type=MESH,
        ).wait_recv()
    for copy in sent + parts:
        copy.wait_send()


def exchange(mine_ref, out_ref, theirs, summed, kpt_sems, freq_send, freq_recv):
    count, me = lax.axis_size("freq"), lax.axis_index("freq")
    others, point = lax.axis_size("kpt"), lax.axis_index("kpt")
    kpt_send, kpt_recv = kpt_sems.at[0], kpt_sems.at[1]
    copies = []
    for j in range(1, others):
        target = lax.rem(point + j, others)
        copy = pltpu.make_async_remote_copy(
            src_ref=mine_ref.at[target],
            dst_ref=theirs.at[j],
            send_sem=kpt_send.at[j],
            recv_sem=kpt_recv.at[j],
            device_id={"kpt": target},
            device_id_type=MESH,
        )
        copy.start()
        copies.append(copy)
    total = mine_ref[point]
    for j in range(1, others):
        copies[j - 1].wait()
        total = total + theirs[j]
    each = summed.shape[1]
    for owner in range(count):
        summed[owner] = total[owner * each : (owner + 1) * each]
    copies = []
    for j in range(1, count):
        target = lax.rem(me + j, count)
        copy = pltpu.make_async_remote_copy(
            src_ref=summed.at[target],
            dst_ref=out_ref.at[me],
            send_sem=freq_send.at[j],
            recv_sem=freq_recv.at[me],
            device_id={"freq": target},
            device_id_type=MESH,
        )
        copy.start()
        copies.append(copy)
    out_ref[me] = summed[me]
    for j in range(1, count):
        source = lax.rem(me + j, count)
        pltpu.make_async_remote_copy(
            src_ref=summed.at[source],
            dst_ref=out_ref.at[source],
            send_sem=freq_send.at[j],
            recv_sem=freq_recv.at[source],
            device_id={"freq": source},
            device_id_type=MESH,
        ).wait_recv()
    for copy in copies:
        copy.wait_send()


def whole_kernel(
    points, kweight, proj_ref, sig_ref, slot_ref, back_ref, energy_ref, out_ref,
    proj_all, sig_all, mine, theirs, summed, mr, mi, pm, gather_sems, kpt_sems, end_sems,
):
    gather(proj_ref, sig_ref, proj_all, sig_all, *(gather_sems.at[i] for i in range(4)))
    value = None
    for point in range(points):
        block = point_blocks(
            point, points, kweight, proj_all[:, point], sig_all, slot_ref, back_ref, energy_ref, mr, mi, pm
        )
        value = block if value is None else value + block
    share = mine.shape[1]
    for part in range(mine.shape[0]):
        mine[part] = value[part * share : (part + 1) * share]
    exchange(mine, out_ref, theirs, summed, kpt_sems, end_sems.at[0], end_sems.at[1])


def local(band_energy, projector, sigma, atom_of_slot, kweight):
    count, others = lax.axis_size("freq"), lax.axis_size("kpt")
    points, rows, bands = projector.shape
    atoms = atom_of_slot.shape[0]
    kinds = 2 * ORBS * ORBS
    slots = sigma.shape[3]
    extra = -slots % 8
    sig = jnp.transpose(sigma.reshape(kinds, slots, count), (2, 1, 0))
    held = atom_of_slot.reshape(count, slots)
    if extra:
        sig = jnp.pad(sig, ((0, 0), (0, extra), (0, 0)))
        held = jnp.pad(held, ((0, 0), (0, extra)), constant_values=-1)
    order = atom_of_slot.reshape(count, others, -1).transpose(1, 0, 2).reshape(1, atoms)
    each = atoms // (count * others)
    padded = -(-rows // 16) * 16
    f32 = jnp.float32
    vmem = pl.BlockSpec(memory_space=pltpu.VMEM)
    owned = pl.pallas_call(
        functools.partial(whole_kernel, points),
        out_shape=jax.ShapeDtypeStruct((count, each, kinds), f32),
        in_specs=[pl.BlockSpec(memory_space=pltpu.SMEM)] + [vmem] * 5,
        out_specs=vmem,
        scratch_shapes=[
            pltpu.VMEM((count, points, padded, bands), projector.dtype),
            pltpu.VMEM(sig.shape, f32),
            pltpu.VMEM((others, atoms // others, kinds), f32),
            pltpu.VMEM((others, atoms // others, kinds), f32),
            pltpu.VMEM((count, each, kinds), f32),
            pltpu.VMEM((bands, bands), f32),
            pltpu.VMEM((bands, bands), f32),
            pltpu.VMEM((ORBS * atoms, bands), jnp.bfloat16),
            pltpu.SemaphoreType.DMA((4, count)),
            pltpu.SemaphoreType.DMA((2, others)),
            pltpu.SemaphoreType.DMA((2, count)),
        ],
        compiler_params=pltpu.CompilerParams(
            collective_id=0, has_side_effects=True, vmem_limit_bytes=56 * 1024 * 1024
        ),
        name="whole",
    )(kweight, projector, sig, held.reshape(1, -1), order, band_energy)
    return jnp.transpose(owned, (2, 1, 0)).reshape(2, ORBS, ORBS, -1, count)


def solution(mesh):
    placed = (P("kpt", None), P("kpt", "freq", None), P(None, None, None, "freq", None), P(), P())
    return jax.shard_map(
        local,
        mesh=mesh,
        in_specs=placed,
        out_specs=P(None, None, None, ("freq", "kpt"), None),
        check_vma=False,
    )
```

```python
import functools
import math

import jax
import jax.numpy as jnp
from jax import lax
from jax.experimental import pallas as pl
from jax.experimental.pallas import tpu as pltpu
from jax.sharding import PartitionSpec as P

ORBS = 5
TILE = 128
MESH = pl.DeviceIdType.MESH
STEP = 64

HIGH = lax.Precision.HIGHEST
BETA_INV = 0.1

OUTER = (((0,), (0,)), ((), ()))
ROWS = (((1,), (1,)), ((), ()))


def halves(value):
    top = value.astype(jnp.bfloat16)
    return top, (value - top.astype(jnp.float32)).astype(jnp.bfloat16)


def dot(a, b, dims=(((1,), (0,)), ((), ()))):
    return lax.dot_general(a, b, dims, preferred_element_type=jnp.float32)


def times(a, b):
    return a[0] * b[0] - a[1] * b[1], a[0] * b[1] + a[1] * b[0]


def plus(a, b):
    return a[0] + b[0], a[1] + b[1]


def minus(a, b):
    return a[0] - b[0], a[1] - b[1]


def pair_inverse(a, b, d):
    det = minus(times(a, d), times(b, b))
    scale = 1.0 / (det[0] * det[0] + det[1] * det[1])
    turned = (det[0] * scale, -det[1] * scale)
    low = times(b, turned)
    return times(d, turned), (-low[0], -low[1]), times(a, turned)


def quad_inverse(e):
    a, b, d = pair_inverse(e[0][0], e[1][0], e[1][1])
    t = [[plus(times(x, e[j][0]), times(y, e[j][1])) for j in (2, 3)] for x, y in ((a, b), (b, d))]
    rest = {}
    for i in (2, 3):
        for j in (2, 3):
            if j <= i:
                taken = plus(times(e[i][0], t[0][j - 2]), times(e[i][1], t[1][j - 2]))
                rest[i, j] = minus(e[i][j], taken)
    f, g, h = pair_inverse(rest[2, 2], rest[3, 2], rest[3, 3])
    n = [[plus(times(p[0], x), times(p[1], y)) for x, y in ((f, g), (g, h))] for p in t]
    top = [
        plus(a, plus(times(n[0][0], t[0][0]), times(n[0][1], t[0][1]))),
        plus(b, plus(times(n[0][0], t[1][0]), times(n[0][1], t[1][1]))),
        plus(d, plus(times(n[1][0], t[1][0]), times(n[1][1], t[1][1]))),
    ]
    neg = [[(-x[0], -x[1]) for x in line] for line in n]
    return [
        [top[0], top[1], neg[0][0], neg[0][1]],
        [top[1], top[2], neg[1][0], neg[1][1]],
        [neg[0][0], neg[1][0], f, g],
        [neg[0][1], neg[1][1], g, h],
    ]


def small_inverse(real, imag):
    size = real.shape[0]
    shape = (8, size)
    lanes = lax.broadcasted_iota(jnp.int32, shape, 1)
    rows = lax.broadcasted_iota(jnp.int32, shape, 0)
    parts = [
        [(m[h : h + 8, :]) for m in (real, imag)] for h in range(0, size, 8)
    ]
    for k in range(0, size, 4):
        own, off = k // 8, k % 8
        here = (lanes >= k) & (lanes < k + 4)
        down = (rows >= off) & (rows < off + 4)
        cols = [
            [
                tuple(jnp.broadcast_to(m[:, k + j : k + j + 1], shape) for m in part)
                for part in parts
            ]
            for j in range(4)
        ]
        e = [
            [
                tuple(jnp.broadcast_to(m[off + i : off + i + 1, :], shape) for m in cols[j][own])
                for j in range(i + 1)
            ]
            for i in range(4)
        ]
        line = []
        for i in range(4):
            r, v = (jnp.broadcast_to(m[off + i : off + i + 1, :], shape) for m in parts[own])
            line.append(
                (
                    jnp.where(here, (lanes == k + i).astype(jnp.float32), r),
                    jnp.where(here, 0.0, v),
                )
            )
        inverse = quad_inverse(e)
        solved = []
        for i in range(4):
            value = times(inverse[i][0], line[0])
            for j in range(1, 4):
                value = plus(value, times(inverse[i][j], line[j]))
            solved.append(value)
        fresh = []
        for h, part in enumerate(parts):
            gone = here | down if h == own else here
            value = tuple(jnp.where(gone, 0.0, m) for m in part)
            for j in range(4):
                col = cols[j][h]
                if h == own:
                    col = (
                        jnp.where(down, (rows == off + j).astype(jnp.float32), col[0]),
                        jnp.where(down, 0.0, col[1]),
                    )
                value = minus(value, times(col, solved[j]))
            fresh.append(value)
        parts = fresh
    return tuple(jnp.concatenate([p[x] for p in parts], axis=0) for x in range(2))


def sweep(mr, mi, bands):
    eye = (
        lax.broadcasted_iota(jnp.int32, (STEP, STEP), 0)
        == lax.broadcasted_iota(jnp.int32, (STEP, STEP), 1)
    ).astype(jnp.float32)
    lane = lax.broadcasted_iota(jnp.int32, (STEP, TILE), 1)
    row = lax.broadcasted_iota(jnp.int32, (STEP, TILE), 0)
    wide = lax.broadcasted_iota(jnp.int32, (1, bands), 1)

    def tile_step(tile, carry):
        base = pl.multiple_of(tile * TILE, TILE)
        for part in range(TILE // STEP):
            off = part * STEP
            start = pl.multiple_of(base + off, STEP)
            own = pl.ds(start, STEP)
            cols = pl.ds(base, TILE)
            dr = mr[own, cols][:, off : off + STEP]
            di = mi[own, cols][:, off : off + STEP]
            nr, ni = small_inverse(dr, di)
            vr, vi = -nr, -ni
            place = wide - start
            inside = (place >= 0) & (place < STEP)
            unit = (
                lax.broadcasted_iota(jnp.int32, (STEP, bands), 1)
                == lax.broadcasted_iota(jnp.int32, (STEP, bands), 0) + start
            ).astype(jnp.float32)
            rr = jnp.where(inside, unit, mr[own, :])
            ri = jnp.where(inside, 0.0, mi[own, :])
            rrh, rrl = halves(rr)
            rih, ril = halves(ri)
            stack = jnp.concatenate([rrh, rrh, rrl, rih, rih, ril], axis=0)
            vrh, vrl = halves(vr)
            vih, vil = halves(vi)
            left = jnp.concatenate(
                [
                    jnp.concatenate([vrh, vrl, vrh, -vih, -vil, -vih], axis=0),
                    jnp.concatenate([vih, vil, vih, vrh, vrl, vrh], axis=0),
                ],
                axis=1,
            )
            both = dot(left, stack, OUTER)
            qr, qi = both[:STEP], both[STEP:]
            qrh, qrl = halves(qr)
            qih, qil = halves(qi)
            to_real = jnp.concatenate([qrh, qrl, qrh, -qih, -qil, -qih], axis=0)
            to_imag = jnp.concatenate([qih, qil, qih, qrh, qrl, qrh], axis=0)
            mr[...] = jnp.where(inside, 0.0, mr[...]) - dot(stack, to_real, OUTER)
            mi[...] = jnp.where(inside, 0.0, mi[...]) - dot(stack, to_imag, OUTER)
            mr[own, :] = -qr
            mi[own, :] = -qi
        return carry

    lax.fori_loop(0, bands // TILE, tile_step, 0)


def point_blocks(point, points, kweight, proj, sig_all, slot_ref, back_ref, energy_ref, mr, mi, pm):
    atoms = back_ref.shape[1]
    owners, padded, bands = proj.shape
    each = atoms // owners
    omega = (2 * lax.axis_index("freq") + 1).astype(jnp.float32) * (math.pi * BETA_INV)
    count = kweight.shape[0]
    total = sum(kweight[i] for i in range(count)).astype(jnp.float32)
    weight = kweight[lax.axis_index("kpt") * points + point].astype(jnp.float32)
    rows = lax.broadcasted_iota(jnp.int32, (atoms, atoms), 0)
    cols = lax.broadcasted_iota(jnp.int32, (atoms, atoms), 1)
    eye = rows == cols
    held = slot_ref.shape[1]
    turn = (lax.broadcasted_iota(jnp.int32, (atoms, held), 0) == slot_ref[...]).astype(jnp.float32)
    sig = sig_all[...].reshape(held, sig_all.shape[2])
    sig = jnp.dot(turn, sig, precision=HIGH, preferred_element_type=jnp.float32).T

    proj = proj.reshape(owners * padded, bands)
    orow = lax.broadcasted_iota(jnp.int32, (atoms, owners * padded), 0)
    ocol = lax.broadcasted_iota(jnp.int32, (atoms, owners * padded), 1)
    target = ocol - (lax.div(orow, each) * padded + lax.rem(orow, each) * ORBS)
    for m in range(ORBS):
        pick = (target == m).astype(jnp.float32).astype(jnp.bfloat16)
        pm[m * atoms : (m + 1) * atoms, :] = dot(pick, proj).astype(jnp.bfloat16)
    planes = pm[...]

    def lifted(first):
        made = []
        for m in range(ORBS):
            line = [
                jnp.where(eye, sig[first + m * ORBS + o : first + m * ORBS + o + 1, :], 0.0)
                for o in range(ORBS)
            ]
            high, low = halves(jnp.concatenate(line, axis=1))
            made.append((dot(high, planes) + dot(low, planes)).astype(jnp.bfloat16))
        made = jnp.concatenate(made, axis=0)
        return dot(
            jnp.concatenate([planes, made], axis=0), jnp.concatenate([made, planes], axis=0), OUTER
        )

    diag = lax.broadcasted_iota(jnp.int32, (bands, bands), 0) == lax.broadcasted_iota(
        jnp.int32, (bands, bands), 1
    )
    mr[...] = -jnp.where(diag, energy_ref[point : point + 1, :], 0.0) - 0.5 * lifted(0)
    mi[...] = jnp.where(diag, omega, 0.0) - 0.5 * lifted(ORBS * ORBS)

    sweep(mr, mi, bands)

    lines = {}
    for which, ref in enumerate((mr, mi)):
        high, low = halves(ref[...])
        spread = dot(planes, high) + dot(planes, low)
        for m in range(ORBS):
            vh, vl = halves(spread[m * atoms : (m + 1) * atoms, :])
            rest = planes[m * atoms :, :]
            block = dot(vh, rest, ROWS) + dot(vl, rest, ROWS)
            for o in range(m, ORBS):
                part = block[:, (o - m) * atoms : (o - m + 1) * atoms]
                lines[which, m, o] = lines[which, o, m] = jnp.sum(
                    jnp.where(eye, part, 0.0), axis=0, keepdims=True
                )
    lines = [lines[w, m, o] for w in range(2) for m in range(ORBS) for o in range(ORBS)]
    scale = jnp.full((1, 1), weight) / jnp.full((1, 1), total)
    found = jnp.concatenate(lines, axis=0) * -scale
    back = (rows == back_ref[...]).astype(jnp.float32)
    return jnp.dot(found, back, precision=HIGH, preferred_element_type=jnp.float32).T


def radices(count):
    made = []
    for radix in (2, 2):
        if count % radix == 0:
            made.insert(0, radix)
            count //= radix
    while count > 1:
        radix = 4 if count % 4 == 0 else count
        made.insert(0, radix)
        count //= radix
    return made


def others_of():
    count, me = lax.axis_size("freq"), lax.axis_index("freq")
    points, point = lax.axis_size("kpt"), lax.axis_index("kpt")
    return [
        (lax.rem(me + j, count), lax.rem(point + p, points))
        for j in range(count)
        for p in range(points)
        if j + p > 0
    ]


def gather(proj_ref, sig_ref, proj_out, sig_out, proj_send, proj_recv, sig_send, sig_recv):
    count, me = lax.axis_size("freq"), lax.axis_index("freq")
    barrier = pltpu.get_barrier_semaphore()
    peers = others_of()
    for freq, kpt in peers:
        pl.semaphore_signal(
            barrier, inc=1, device_id={"freq": freq, "kpt": kpt}, device_id_type=MESH
        )
    points, rows, bands = proj_ref.shape
    padded = proj_out.shape[2]
    own = proj_ref[...]
    if padded > rows:
        own = jnp.concatenate([own, jnp.zeros((points, padded - rows, bands), own.dtype)], axis=1)
    proj_out[me] = own
    sig_out[me] = sig_ref[me]
    pl.semaphore_wait(barrier, len(peers))

    dims = radices(count)
    strides = [math.prod(dims[s + 1 :]) for s in range(len(dims))]

    def shifted(index, s, j):
        digit = lax.rem(lax.div(index, strides[s]), dims[s])
        return index + (lax.rem(digit + j, dims[s]) - digit) * strides[s]

    def block(owner, target, slot):
        return pltpu.make_async_remote_copy(
            src_ref=proj_out.at[owner],
            dst_ref=proj_out.at[owner],
            send_sem=proj_send.at[slot],
            recv_sem=proj_recv.at[owner],
            device_id={"freq": target},
            device_id_type=MESH,
        )

    sent = []

    def forward(owner, first):
        for s in range(first, len(dims)):
            for j in range(1, dims[s]):
                copy = block(owner, shifted(me, s, j), len(sent))
                copy.start()
                sent.append(copy)

    forward(me, 0)
    parts = []
    for j in range(1, count):
        target = lax.rem(me + j, count)
        copy = pltpu.make_async_remote_copy(
            src_ref=sig_ref.at[target],
            dst_ref=sig_out.at[me],
            send_sem=sig_send.at[j],
            recv_sem=sig_recv.at[me],
            device_id={"freq": target},
            device_id_type=MESH,
        )
        copy.start()
        parts.append(copy)
    got = [me]
    for s in range(len(dims)):
        fresh = []
        for j in range(1, dims[s]):
            for base in got:
                owner = shifted(base, s, j)
                block(owner, owner, 0).wait_recv()
                forward(owner, s + 1)
                fresh.append(owner)
        got += fresh
    for j in range(1, count):
        source = lax.rem(me + j, count)
        pltpu.make_async_remote_copy(
            src_ref=sig_ref.at[source],
            dst_ref=sig_out.at[source],
            send_sem=sig_send.at[j],
            recv_sem=sig_recv.at[source],
            device_id={"freq": source},
            device_id_type=MESH,
        ).wait_recv()
    for copy in sent + parts:
        copy.wait_send()


def exchange(mine, landed, out_ref, sends, recvs):
    me, point = lax.axis_index("freq"), lax.axis_index("kpt")

    def part(freq, kpt, to_freq, to_kpt):
        return pltpu.make_async_remote_copy(
            src_ref=mine.at[to_kpt, to_freq],
            dst_ref=landed.at[kpt, freq],
            send_sem=sends.at[to_kpt, to_freq],
            recv_sem=recvs.at[kpt, freq],
            device_id={"freq": to_freq, "kpt": to_kpt},
            device_id_type=MESH,
        )

    peers = others_of()
    copies = [part(me, point, *peer) for peer in peers]
    for copy in copies:
        copy.start()
    landed[point, me] = mine[point, me]
    for freq, kpt in peers:
        part(freq, kpt, freq, kpt).wait_recv()
    total = landed[0]
    for kpt in range(1, landed.shape[0]):
        total = total + landed[kpt]
    out_ref[...] = total
    for copy in copies:
        copy.wait_send()


def whole_kernel(
    points, kweight, proj_ref, sig_ref, slot_ref, back_ref, energy_ref, out_ref,
    proj_all, sig_all, mine, landed, mr, mi, pm, gather_sems, end_sems,
):
    gather(proj_ref, sig_ref, proj_all, sig_all, *(gather_sems.at[i] for i in range(4)))
    value = None
    for point in range(points):
        block = point_blocks(
            point, points, kweight, proj_all[:, point], sig_all, slot_ref, back_ref, energy_ref, mr, mi, pm
        )
        value = block if value is None else value + block
    parts, owners, each, _ = mine.shape
    for part in range(parts):
        for owner in range(owners):
            first = (part * owners + owner) * each
            mine[part, owner] = value[first : first + each]
    exchange(mine, landed, out_ref, end_sems.at[0], end_sems.at[1])


def local(band_energy, projector, sigma, atom_of_slot, kweight):
    count, others = lax.axis_size("freq"), lax.axis_size("kpt")
    points, rows, bands = projector.shape
    atoms = atom_of_slot.shape[0]
    kinds = 2 * ORBS * ORBS
    slots = sigma.shape[3]
    extra = -slots % 8
    sig = jnp.transpose(sigma.reshape(kinds, slots, count), (2, 1, 0))
    held = atom_of_slot.reshape(count, slots)
    if extra:
        sig = jnp.pad(sig, ((0, 0), (0, extra), (0, 0)))
        held = jnp.pad(held, ((0, 0), (0, extra)), constant_values=-1)
    order = atom_of_slot.reshape(count, others, -1).transpose(1, 0, 2).reshape(1, atoms)
    each = atoms // (count * others)
    padded = -(-rows // 16) * 16
    f32 = jnp.float32
    vmem = pl.BlockSpec(memory_space=pltpu.VMEM)
    owned = pl.pallas_call(
        functools.partial(whole_kernel, points),
        out_shape=jax.ShapeDtypeStruct((count, each, kinds), f32),
        in_specs=[pl.BlockSpec(memory_space=pltpu.SMEM)] + [vmem] * 5,
        out_specs=vmem,
        scratch_shapes=[
            pltpu.VMEM((count, points, padded, bands), projector.dtype),
            pltpu.VMEM(sig.shape, f32),
            pltpu.VMEM((others, count, each, kinds), f32),
            pltpu.VMEM((others, count, each, kinds), f32),
            pltpu.VMEM((bands, bands), f32),
            pltpu.VMEM((bands, bands), f32),
            pltpu.VMEM((ORBS * atoms, bands), jnp.bfloat16),
            pltpu.SemaphoreType.DMA((4, count)),
            pltpu.SemaphoreType.DMA((2, others, count)),
        ],
        compiler_params=pltpu.CompilerParams(
            collective_id=0, has_side_effects=True, vmem_limit_bytes=56 * 1024 * 1024
        ),
        name="whole",
    )(kweight, projector, sig, held.reshape(1, -1), order, band_energy)
    return jnp.transpose(owned, (2, 1, 0)).reshape(2, ORBS, ORBS, -1, count)


def solution(mesh):
    placed = (P("kpt", None), P("kpt", "freq", None), P(None, None, None, "freq", None), P(), P())
    return jax.shard_map(
        local,
        mesh=mesh,
        in_specs=placed,
        out_specs=P(None, None, None, ("freq", "kpt"), None),
        check_vma=False,
    )
```
